256 devices in a mesh: ctx: 64 (over z, y, core), tp: 4 (over x).
Axes of the slice: x: 4, y: 4, z: 8, core: 2. Of those that a mesh axis runs over, the one named last changes fastest.
Arguments:
- gate_query: bfloat16 [16384, 4096], P('ctx', 'tp'), may hold values from -6 to 6
- gate_key: bfloat16 [16384, 4096], P('ctx', 'tp'), may hold values from -6 to 6
- value_in: bfloat16 [16384, 4096], P('ctx', 'tp'), may hold values from -6 to 6
- residues: float32 [4096, 16], P('tp'), may hold values from -1.5 to 1.5
- decay_rate: float32 [4096, 16], P('tp'), may hold values from 6.1035156e-05 to 0.03
- skip_gain: float32 [4096], P('tp'), may hold values from -4 to 4
- out_weight: bfloat16 [4096, 4096], P('tp'), may hold values from -0.09375 to 0.09375
Outputs:
- mixed: bfloat16 [16384, 4096], P('ctx', 'tp')
The draws below stay inside these ranges and needn't reach their ends.
All inputs are finite; a program needn't handle non-finite values.
Results may differ from the reference program's by a relative error of at most 0.02.
Values may be sent and summed in bfloat16 or wider, within the bound.
No kernel may reach another device: no remote copies, remote signals or barrier semaphores. Data moves between devices by JAX's collectives and lax.ppermute only.
A program may use at most 128 MiB of HBM per device.

```python
import math
import jax
import jax.numpy as jnp
from jax import lax

C_IN = 4096
D_OUT = 4096
ORDER = 16
SEQ = 16384


def level_of(rng, extent, cuts, least, high):
    factor_of = 1.0
    for dim, parts in cuts:
        heights = jax.random.uniform(jax.random.fold_in(jax.random.fold_in(rng, 6), dim), (parts,), jnp.float32, least / len(cuts), high / len(cuts))
        factor_of = factor_of * jnp.repeat(jnp.exp(heights), extent[dim] // parts).reshape((-1,) + (1,) * (len(extent) - 1 - dim))
    return factor_of


def normal_values(rng, dims, deviation, most, cuts=(), kind=jnp.bfloat16):
    drawn = deviation * jax.random.normal(rng, dims, jnp.float32)
    if cuts:
        drawn = drawn * level_of(rng, dims, cuts, -0.22, 0.18)
    return jnp.clip(drawn, -most, most).astype(kind)


def setup_inputs(seed: int = 0) -> dict:
    key_of = jax.random.split(jax.random.key(seed), 8)
    return {
        "gate_query": normal_values(key_of[0], (SEQ, C_IN), 1.0, 6.0, ((0, 64), (1, 4))),
        "gate_key": normal_values(key_of[1], (SEQ, C_IN), 1.0, 6.0, ((0, 64), (1, 4))),
        "value_in": normal_values(key_of[2], (SEQ, C_IN), 1.0, 6.0, ((0, 64), (1, 4))),
        "residues": normal_values(key_of[3], (C_IN, ORDER), 0.25, 1.5, ((0, 4),), jnp.float32),
        "decay_rate": jnp.clip(jnp.exp(math.log(0.03) - 6.1975026 * jax.random.uniform(key_of[4], (C_IN, ORDER), jnp.float32) ** level_of(key_of[4], (C_IN, ORDER), ((0, 4),), -0.2, 0.2)), 6.103515625e-05, 0.03),
        "skip_gain": normal_values(key_of[5], (C_IN,), 1.0, 4.0, ((0, 4),), jnp.float32),
        "out_weight": normal_values(key_of[6], (C_IN, D_OUT), C_IN ** -0.5, 0.09375, ((0, 4),)),
    }


def block_conv(pieces):
    keyed_block, res_block, dec_block = pieces
    steps = jnp.arange(SEQ).astype(jnp.float32)
    filt = jnp.zeros(keyed_block.shape, jnp.float32)
    for mode in range(ORDER):
        decay = dec_block[:, mode]
        scale = res_block[:, mode] * jnp.sqrt(-jnp.expm1(-2.0 * decay))
        filt = filt + scale[None, :] * jnp.exp(-decay[None, :] * steps[:, None])
    spec_filt = jnp.fft.rfft(filt, n=2 * SEQ, axis=0)
    spec_keyed = jnp.fft.rfft(keyed_block, n=2 * SEQ, axis=0)
    return jnp.fft.irfft(spec_filt * spec_keyed, n=2 * SEQ, axis=0)[:SEQ].astype(keyed_block.dtype)

def reference(gate_query, gate_key, value_in, residues, decay_rate, skip_gain, out_weight):
    keyed = gate_key.astype(jnp.float32) * value_in.astype(jnp.float32)
    width = min(256, C_IN)
    blocks = C_IN // width
    keyed_blocks = keyed.reshape(SEQ, blocks, width).transpose(1, 0, 2)
    res_blocks = residues.reshape(blocks, width, ORDER)
    dec_blocks = decay_rate.reshape(blocks, width, ORDER)
    conv = lax.map(block_conv, (keyed_blocks, res_blocks, dec_blocks))
    conv = conv.transpose(1, 0, 2).reshape(SEQ, C_IN)
    gated = (gate_query.astype(jnp.float32) * (conv + skip_gain[None, :] * keyed)).astype(jnp.bfloat16)
    mixed = jnp.dot(gated.astype(jnp.float32), out_weight.astype(jnp.float32), precision=lax.Precision.HIGHEST)
    return mixed.astype(jnp.bfloat16)
```

```python
import functools

import jax
import jax.numpy as jnp
from jax import lax
from jax.experimental import pallas as pl
from jax.experimental.pallas import tpu as pltpu
from jax.sharding import PartitionSpec as P

MODES = 16
LANES = 128
SUB = 8
ROWS = 16


def local_kernel(key_ref, value_ref, decay_ref, scale_ref, skip_ref, local_ref, state_ref, keyed_ref):
    groups = key_ref.shape[1] // LANES
    span = groups * SUB
    length = key_ref.shape[0]
    step = [jnp.exp(-decay_ref[r]) for r in range(MODES)]
    scale = [scale_ref[r] for r in range(MODES)]
    skip = skip_ref[...]

    def block(i, held):
        rows = pl.ds(pl.multiple_of(i * ROWS, ROWS), ROWS)
        keyed = key_ref[rows, :].astype(jnp.float32) * value_ref[rows, :].astype(jnp.float32)
        for half in range(ROWS // SUB):
            base = (i * (ROWS // SUB) + half) * span
            for g in range(groups):
                keyed_ref[pl.ds(pl.multiple_of(base + g * SUB, SUB), SUB), :] = keyed[
                    half * SUB : (half + 1) * SUB, g * LANES : (g + 1) * LANES
                ]
        for half in range(ROWS // SUB):
            base = (i * (ROWS // SUB) + half) * span
            for s in range(SUB):
                at = pl.ds(base + s, groups, stride=SUB)
                now = keyed_ref[at, :]
                held = [a * h + now for a, h in zip(step, held)]
                terms = [c * h for c, h in zip(scale, held)] + [skip * now]
                while len(terms) > 1:
                    terms = [sum(terms[j : j + 2]) for j in range(0, len(terms), 2)]
                local_ref[at, :] = terms[0]
        return held

    held = lax.fori_loop(0, length // ROWS, block, [jnp.zeros((groups, LANES), jnp.float32)] * MODES)
    for r in range(MODES):
        state_ref[r] = held[r]


def local_part(gate_key, value_in, decay, scale, skip):
    length, chans = gate_key.shape
    groups = chans // LANES
    return pl.pallas_call(
        local_kernel,
        out_shape=(
            jax.ShapeDtypeStruct((length * groups, LANES), jnp.float32),
            jax.ShapeDtypeStruct((MODES, groups, LANES), jnp.float32),
        ),
        scratch_shapes=[pltpu.VMEM((length * groups, LANES), jnp.float32)],
        compiler_params=pltpu.CompilerParams(vmem_limit_bytes=32 * 2**20),
        cost_estimate=pl.CostEstimate(flops=8 * 2**20, bytes_accessed=2 * 2**20, transcendentals=0),
    )(gate_key, value_in, decay, scale, skip)


def carry_kernel(place_ref, local_ref, query_ref, decay_ref, scale_ref, carry_ref, weight_ref,
                 gated_ref, part_ref, tail_ref, weight_buf, sem):
    length, chans = query_ref.shape
    groups = chans // LANES
    span = groups * SUB
    width = part_ref.shape[1]
    fetch = pltpu.make_async_copy(
        weight_ref.at[:, pl.ds(pl.multiple_of(place_ref[0] * width, width), width)], weight_buf, sem
    )
    fetch.start()
    step = [jnp.exp(-decay_ref[r]) for r in range(MODES)]
    start = [scale_ref[r] * step[r] * carry_ref[r] for r in range(MODES)]

    def block(i, held):
        rows = pl.ds(pl.multiple_of(i * ROWS, ROWS), ROWS)
        for half in range(ROWS // SUB):
            for s in range(SUB):
                terms = held
                while len(terms) > 1:
                    terms = [sum(terms[j : j + 2]) for j in range(0, len(terms), 2)]
                tail_ref[pl.ds(half * span + s, groups, stride=SUB), :] = terms[0]
                held = [a * h for a, h in zip(step, held)]
        for g in range(groups):
            parts = []
            for half in range(ROWS // SUB):
                base = (i * (ROWS // SUB) + half) * span + g * SUB
                parts.append(
                    local_ref[pl.ds(pl.multiple_of(base, SUB), SUB), :]
                    + tail_ref[half * span + g * SUB : half * span + (g + 1) * SUB, :]
                )
            mixing = jnp.concatenate(parts, axis=0)
            cols = slice(g * LANES, (g + 1) * LANES)
            gated_ref[rows, cols] = (query_ref[rows, cols].astype(jnp.float32) * mixing).astype(
                jnp.bfloat16
            )
        return held

    lax.fori_loop(0, length // ROWS, block, start)
    fetch.wait()
    part_ref[...] = jnp.dot(
        gated_ref[...], weight_buf[...], preferred_element_type=jnp.float32
    ).astype(jnp.bfloat16)


VMEM = pl.BlockSpec(memory_space=pltpu.VMEM)


def carry_part(place, local, gate_query, decay, scale, carry, weight):
    length, chans = gate_query.shape
    groups = chans // LANES
    width = weight.shape[1] // 4
    return pl.pallas_call(
        carry_kernel,
        out_shape=(
            jax.ShapeDtypeStruct((length, chans), jnp.bfloat16),
            jax.ShapeDtypeStruct((length, width), jnp.bfloat16),
        ),
        in_specs=[pl.BlockSpec(memory_space=pltpu.SMEM)] + [VMEM] * 5 + [pl.BlockSpec(memory_space=pl.ANY)],
        out_specs=(VMEM, VMEM),
        scratch_shapes=[
            pltpu.VMEM((ROWS * groups, LANES), jnp.float32),
            pltpu.VMEM((chans, width), jnp.bfloat16),
            pltpu.SemaphoreType.DMA,
        ],
        compiler_params=pltpu.CompilerParams(vmem_limit_bytes=32 * 2**20),
        cost_estimate=pl.CostEstimate(flops=2**30, bytes_accessed=5 * 2**20, transcendentals=0),
    )(place, local, gate_query, decay, scale, carry, weight)


def project_kernel(place_ref, gated_ref, weight_ref, out_ref):
    out_ref[...] = jnp.dot(gated_ref[...], weight_ref[...], preferred_element_type=jnp.float32)[None]


def project(places, gated, weight):
    length, chans = gated.shape
    width = weight.shape[1] // 4
    count = places.shape[0]
    return pl.pallas_call(
        project_kernel,
        out_shape=jax.ShapeDtypeStruct((count, length, width), jnp.float32),
        grid_spec=pltpu.PrefetchScalarGridSpec(
            num_scalar_prefetch=1,
            grid=(count,),
            in_specs=[
                pl.BlockSpec((length, chans), lambda i, p: (0, 0)),
                pl.BlockSpec((chans, width), lambda i, p: (0, p[i])),
            ],
            out_specs=pl.BlockSpec((1, length, width), lambda i, p: (i, 0, 0)),
        ),
        compiler_params=pltpu.CompilerParams(vmem_limit_bytes=32 * 2**20),
        cost_estimate=pl.CostEstimate(
            flops=2 * count * length * chans * width,
            bytes_accessed=2 * count * chans * width,
            transcendentals=0,
        ),
    )(places, gated, weight)


def scan_over_ctx(state, decay, length, index):
    groups = lax.axis_size("ctx")

    def power(blocks):
        blocks = jnp.asarray(blocks)
        return jnp.where(blocks >= 0, jnp.exp(-decay * (length * jnp.maximum(blocks, 0)).astype(jnp.float32)), 0.0)

    total, before = state, jnp.zeros_like(state)
    span = 1
    for bits in (1, 2, 1, 2):
        members = 1 << bits
        mine = index // span % members
        inside = index % span
        sent = total.astype(jnp.bfloat16)
        got = [(0, total)]
        for k in range(1, members):
            pairs = [(i, i ^ (k * span)) for i in range(groups)]
            got.append((k, lax.ppermute(sent, "ctx", pairs).astype(jnp.float32)))
        for k, theirs in got[1:]:
            other = mine ^ k
            before = before + theirs * power(
                jnp.where(other < mine, (mine - 1 - other) * span + inside, -1)
            )
        total = sum(theirs * power((members - 1 - (mine ^ k)) * span) for k, theirs in got)
        span *= members
    return before


def on_device(gate_query, gate_key, value_in, residues, decay_rate, skip_gain, out_weight):
    index = lax.axis_index("ctx")
    mine = lax.axis_index("tp")
    length, chans = gate_key.shape
    groups = chans // LANES
    decay = decay_rate.T.reshape(MODES, groups, LANES)
    scale = residues.T.reshape(MODES, groups, LANES) * jnp.sqrt(-jnp.expm1(-2.0 * decay))
    skip = skip_gain.reshape(groups, LANES)
    local, state = local_part(gate_key, value_in, decay, scale, skip)
    carry = scan_over_ctx(state, decay, length, index)

    ring = lax.axis_size("tp")
    after, prior = (mine + 1) % ring, (mine + ring - 1) % ring
    far = (mine + 2) % ring
    forth = [(i, (i + 1) % ring) for i in range(ring)]
    back = [(i, (i + ring - 1) % ring) for i in range(ring)]
    half = length // 2
    gated, far_part = carry_part(far[None], local, gate_query, decay, scale, carry, out_weight)
    far_a = lax.ppermute(far_part[:half], "tp", forth)
    far_b = lax.ppermute(far_part[half:], "tp", back)
    parts = project(jnp.stack([after, prior, mine]), gated, out_weight)
    near_b = lax.ppermute(parts[0, half:].astype(jnp.bfloat16), "tp", forth)
    near_a = lax.ppermute(parts[1, :half].astype(jnp.bfloat16), "tp", back)
    both_a = lax.ppermute((parts[0, :half] + far_a.astype(jnp.float32)).astype(jnp.bfloat16), "tp", forth)
    both_b = lax.ppermute((parts[1, half:] + far_b.astype(jnp.float32)).astype(jnp.bfloat16), "tp", back)
    first = parts[2, :half] + near_a.astype(jnp.float32) + both_a.astype(jnp.float32)
    second = parts[2, half:] + near_b.astype(jnp.float32) + both_b.astype(jnp.float32)
    return jnp.concatenate([first, second]).astype(jnp.bfloat16)


def solution(mesh):
    in_specs = (
        P("ctx", "tp"),
        P("ctx", "tp"),
        P("ctx", "tp"),
        P("tp", None),
        P("tp", None),
        P("tp"),
        P("tp", None),
    )
    return jax.shard_map(
        on_device, mesh=mesh, in_specs=in_specs, out_specs=P("ctx", "tp"), check_vma=False
    )
```

```python
import functools

import jax
import jax.numpy as jnp
from jax import lax
from jax.experimental import pallas as pl
from jax.experimental.pallas import tpu as pltpu
from jax.sharding import PartitionSpec as P

MODES = 16
LANES = 128
SUB = 8
ROWS = 16


CHUNKS = 4
FAR, AFTER, PRIOR, MINE = 2, 1, 3, 0
STAGES = (
    (2, ((1, 1),), False),
    (4, ((1, 2), (3, 6), (2, 4)), False),
    (4, ((1, 8), (2, 16), (3, 24)), False),
    (2, ((1, 56),), False),
)
HBM = pl.BlockSpec(memory_space=pltpu.HBM)
VMEM = pl.BlockSpec(memory_space=pltpu.VMEM)
DMA = pltpu.SemaphoreType.DMA


def in_hbm(array):
    return pltpu.with_memory_space_constraint(array, pltpu.HBM)


def params():
    return pltpu.CompilerParams(vmem_limit_bytes=24 * 2**20)


def cost(flops, size):
    return pl.CostEstimate(flops=flops, bytes_accessed=size, transcendentals=0)


def wide(*shape):
    return jax.ShapeDtypeStruct(shape, jnp.float32)


def short(*shape):
    return jax.ShapeDtypeStruct(shape, jnp.bfloat16)


def total_of(terms):
    while len(terms) > 1:
        terms = [sum(terms[j : j + 2]) for j in range(0, len(terms), 2)]
    return terms[0]


def fetch_columns(weight_hbm, turn, out_ref, sems, first=0):
    chans, width = out_ref.shape
    owner = lax.rem(lax.axis_index("tp") + turn, weight_hbm.shape[1] // width)
    columns = pl.ds(pl.multiple_of(owner * width, width), width)
    part = chans // CHUNKS
    copies = []
    for c in range(CHUNKS):
        rows = pl.ds(c * part, part)
        copies.append(
            pltpu.make_async_copy(weight_hbm.at[rows, columns], out_ref.at[rows, :], sems.at[first + c])
        )
        copies[-1].start()
    return copies


def wait_all(copies):
    for copy in copies:
        copy.wait()


def state_kernel(key_hbm, value_hbm, decay_hbm, residue_hbm, skip_hbm,
                 state_ref, keyed_ref, decay_ref, residue_ref, skip_ref,
                 key_buf, value_buf, mode_buf, turn_buf, sems):
    length, chans = key_buf.shape
    groups = chans // LANES
    span = groups * SUB
    part = length // CHUNKS
    small = []
    for n, src in enumerate((decay_hbm, residue_hbm)):
        small.append(pltpu.make_async_copy(src, mode_buf.at[n], sems.at[2 * CHUNKS + n]))
    small[0].start()
    copies = []
    for c in range(CHUNKS):
        rows = pl.ds(c * part, part)
        copies.append((
            pltpu.make_async_copy(key_hbm.at[rows, :], key_buf.at[rows, :], sems.at[2 * c]),
            pltpu.make_async_copy(value_hbm.at[rows, :], value_buf.at[rows, :], sems.at[2 * c + 1]),
        ))
        for copy in copies[-1]:
            copy.start()
    small[1].start()
    skip = pltpu.make_async_copy(skip_hbm, skip_ref, sems.at[2 * CHUNKS + 2])
    skip.start()

    def turn(which, out_ref):
        small[which].wait()
        for m in range(MODES // SUB):
            for g in range(groups):
                turn_buf[(m * groups + g) * SUB : (m * groups + g + 1) * SUB, :] = mode_buf[
                    which, m * SUB : (m + 1) * SUB, g * LANES : (g + 1) * LANES
                ]
        for r in range(MODES):
            out_ref[r] = turn_buf[pl.ds(r // SUB * span + r % SUB, groups, stride=SUB), :]

    turn(0, decay_ref)
    step = [jnp.exp(-decay_ref[r]) for r in range(MODES)]

    def block(i, held):
        rows = pl.ds(pl.multiple_of(i * ROWS, ROWS), ROWS)
        keyed = key_buf[rows, :].astype(jnp.float32) * value_buf[rows, :].astype(jnp.float32)
        for half in range(ROWS // SUB):
            base = (i * (ROWS // SUB) + half) * span
            for g in range(groups):
                keyed_ref[pl.ds(pl.multiple_of(base + g * SUB, SUB), SUB), :] = keyed[
                    half * SUB : (half + 1) * SUB, g * LANES : (g + 1) * LANES
                ]
        for half in range(ROWS // SUB):
            base = (i * (ROWS // SUB) + half) * span
            for s in range(SUB):
                now = keyed_ref[pl.ds(base + s, groups, stride=SUB), :]
                held = [a * h + now for a, h in zip(step, held)]
        return held

    held = [jnp.zeros((groups, LANES), jnp.float32)] * MODES
    for c in range(CHUNKS):
        for copy in copies[c]:
            copy.wait()
        held = lax.fori_loop(c * (part // ROWS), (c + 1) * (part // ROWS), block, held)
    for r in range(MODES):
        state_ref[r] = held[r]
    turn(1, residue_ref)
    skip.wait()


def block_state(gate_key, value_in, decay, residue, skip):
    length, chans = gate_key.shape
    groups = chans // LANES
    modes = wide(MODES, groups, LANES)
    return pl.pallas_call(
        state_kernel,
        out_shape=(modes, wide(length * groups, LANES), modes, modes, wide(groups, LANES)),
        in_specs=[HBM] * 5,
        out_specs=(VMEM,) * 5,
        scratch_shapes=[
            pltpu.VMEM((length, chans), jnp.bfloat16),
            pltpu.VMEM((length, chans), jnp.bfloat16),
            pltpu.VMEM((2, MODES, chans), jnp.float32),
            pltpu.VMEM((MODES * groups, LANES), jnp.float32),
            DMA((2 * CHUNKS + 3,)),
        ],
        compiler_params=params(),
        cost_estimate=cost(2**23, 2**23),
    )(*(in_hbm(x) for x in (gate_key, value_in, decay, residue, skip)))


def local_kernel(keyed_ref, decay_ref, scale_ref, _, skip_ref, local_ref, ahead_ref):
    groups = decay_ref.shape[1]
    span = groups * SUB
    ahead = (3 - lax.axis_index("ctx") // 2 % 4) * 2 * (keyed_ref.shape[0] // groups)
    for r in range(MODES):
        ahead_ref[r] = jnp.exp(-decay_ref[r] * ahead.astype(jnp.float32))
    step = [jnp.exp(-decay_ref[r]) for r in range(MODES)]
    scale = [scale_ref[r] for r in range(MODES)]
    skip = skip_ref[...]

    def block(i, held):
        for s in range(SUB):
            at = pl.ds(i * span + s, groups, stride=SUB)
            now = keyed_ref[at, :]
            held = [a * h + now for a, h in zip(step, held)]
            local_ref[at, :] = total_of([c * h for c, h in zip(scale, held)] + [skip * now])
        return held

    lax.fori_loop(0, keyed_ref.shape[0] // span, block, [jnp.zeros((groups, LANES), jnp.float32)] * MODES)


def local_part(keyed, decay, scale, behind, skip):
    return pl.pallas_call(
        local_kernel,
        out_shape=(wide(*keyed.shape), wide(*decay.shape)),
        in_specs=[VMEM] * 5,
        out_specs=(VMEM, VMEM),
        compiler_params=params(),
        cost_estimate=cost(2**23, 2**22),
    )(keyed, decay, scale, behind, skip)


def fetch_kernel(query_hbm, weight_hbm, _, query_ref, far_ref, sems):
    copies = fetch_columns(weight_hbm, FAR, far_ref, sems)
    copies.append(pltpu.make_async_copy(query_hbm, query_ref, sems.at[CHUNKS]))
    copies[-1].start()
    wait_all(copies)


def fetch(gate_query, weight, behind, ring):
    return pl.pallas_call(
        fetch_kernel,
        out_shape=(short(*gate_query.shape), short(weight.shape[0], weight.shape[1] // ring)),
        in_specs=[HBM, HBM, VMEM],
        out_specs=(VMEM,) * 2,
        scratch_shapes=[DMA((CHUNKS + 1,))],
        compiler_params=params(),
        cost_estimate=cost(2**10, 2**22),
    )(in_hbm(gate_query), in_hbm(weight), behind)


def carry_kernel(local_ref, query_ref, decay_ref, start_ref, far_ref, weight_hbm,
                 gated_ref, far_top, far_low, after_ref, tail_ref, sems):
    copies = fetch_columns(weight_hbm, AFTER, after_ref, sems)
    length, chans = gated_ref.shape
    groups = chans // LANES
    span = groups * SUB
    step = [jnp.exp(-decay_ref[r]) for r in range(MODES)]

    def block(i, held):
        rows = pl.ds(pl.multiple_of(i * ROWS, ROWS), ROWS)
        for half in range(ROWS // SUB):
            for s in range(SUB):
                tail_ref[pl.ds(half * span + s, groups, stride=SUB), :] = total_of(held)
                held = [a * h for a, h in zip(step, held)]
        for g in range(groups):
            parts = []
            for half in range(ROWS // SUB):
                base = (i * (ROWS // SUB) + half) * span + g * SUB
                parts.append(
                    local_ref[pl.ds(pl.multiple_of(base, SUB), SUB), :]
                    + tail_ref[half * span + g * SUB : half * span + (g + 1) * SUB, :]
                )
            cols = slice(g * LANES, (g + 1) * LANES)
            gated_ref[rows, cols] = (
                query_ref[rows, cols].astype(jnp.float32) * jnp.concatenate(parts, axis=0)
            ).astype(jnp.bfloat16)
        return held

    lax.fori_loop(0, length // ROWS, block, [start_ref[r] for r in range(MODES)])
    half = length // 2
    for n, out in enumerate((far_top, far_low)):
        out[...] = jnp.dot(
            gated_ref[n * half : (n + 1) * half, :], far_ref[...], preferred_element_type=jnp.float32
        ).astype(jnp.bfloat16)
    wait_all(copies)


def carry_part(local, query, decay, start, far, weight):
    length, chans = query.shape
    groups = chans // LANES
    part = short(length // 2, far.shape[1])
    return pl.pallas_call(
        carry_kernel,
        out_shape=(short(length, chans), part, part, short(*far.shape)),
        in_specs=[VMEM] * 5 + [HBM],
        out_specs=(VMEM,) * 4,
        scratch_shapes=[pltpu.VMEM((ROWS * groups, LANES), jnp.float32), DMA((CHUNKS,))],
        compiler_params=params(),
        cost_estimate=cost(2**29, 2**20),
    )(local, query, decay, start, far, in_hbm(weight))


def near_kernel(gated_ref, after_ref, weight_hbm, after_top, after_low, prior_top, prior_low, prior_buf, sems):
    half = after_top.shape[0]
    copies = fetch_columns(weight_hbm, PRIOR, prior_buf, sems)
    top, low = slice(0, half), slice(half, 2 * half)
    for out, rows, weight in (
        (after_low, low, after_ref),
        (after_top, top, after_ref),
        (prior_top, top, prior_buf),
        (prior_low, low, prior_buf),
    ):
        if out is prior_top:
            wait_all(copies)
        out[...] = jnp.dot(gated_ref[rows, :], weight[...], preferred_element_type=jnp.float32).astype(out.dtype)


def near_part(gated, after, weight):
    shape = (gated.shape[0] // 2, after.shape[1])
    return pl.pallas_call(
        near_kernel,
        out_shape=(wide(*shape), short(*shape), short(*shape), wide(*shape)),
        in_specs=[VMEM, VMEM, HBM],
        out_specs=(VMEM,) * 4,
        scratch_shapes=[pltpu.VMEM(after.shape, jnp.bfloat16), DMA((CHUNKS,))],
        compiler_params=params(),
        cost_estimate=cost(2**30, 2**20),
    )(gated, after, in_hbm(weight))


def own_kernel(gated_ref, weight_hbm, mine_top, mine_low, mine_buf, sems):
    half = mine_top.shape[0]
    wait_all(fetch_columns(weight_hbm, MINE, mine_buf, sems))
    for n, out in enumerate((mine_top, mine_low)):
        out[...] = jnp.dot(
            gated_ref[n * half : (n + 1) * half, :], mine_buf[...], preferred_element_type=jnp.float32
        )


def own_part(gated, weight, ring):
    length, chans = gated.shape
    width = weight.shape[1] // ring
    part = wide(length // 2, width)
    return pl.pallas_call(
        own_kernel,
        out_shape=(part, part),
        in_specs=[VMEM, HBM],
        out_specs=(VMEM,) * 2,
        scratch_shapes=[pltpu.VMEM((chans, width), jnp.bfloat16), DMA((CHUNKS,))],
        compiler_params=params(),
        cost_estimate=cost(2**29, 2**20),
    )(gated, in_hbm(weight))


def finish_kernel(mine_top, near_top, both_top, mine_low, near_low, both_low, out_hbm, out_buf, sems):
    half = mine_top.shape[0]
    copies = []
    for n, (mine, near, both) in enumerate(
        ((mine_top, near_top, both_top), (mine_low, near_low, both_low))
    ):
        rows = pl.ds(n * half, half)
        out_buf[rows, :] = (
            mine[...] + near[...].astype(jnp.float32) + both[...].astype(jnp.float32)
        ).astype(jnp.bfloat16)
        copies.append(pltpu.make_async_copy(out_buf.at[rows, :], out_hbm.at[rows, :], sems.at[n]))
        copies[-1].start()
    for copy in copies:
        copy.wait()


def finish(*parts):
    half, width = parts[0].shape
    return pl.pallas_call(
        finish_kernel,
        out_shape=short(2 * half, width),
        in_specs=[VMEM] * 6,
        out_specs=HBM,
        scratch_shapes=[pltpu.VMEM((2 * half, width), jnp.bfloat16), DMA((2,))],
        compiler_params=params(),
        cost_estimate=cost(2**19, 2**21),
    )(*parts)


def scan_over_ctx(state, decay, length, index, work, load):
    devices = lax.axis_size("ctx")

    def power(blocks):
        blocks = jnp.asarray(blocks)
        reach = (length * jnp.maximum(blocks, 0)).astype(jnp.float32)
        return jnp.where(blocks >= 0, jnp.exp(-decay * reach), 0.0)

    total, before = state, jnp.zeros_like(state)
    span = 1
    for stage, (members, moves, forward) in enumerate(STAGES):
        mine, inside = index // span % members, index % span
        sent = total.astype(jnp.bfloat16)
        own = work(sent) if stage == 1 else power((members - 1 - mine) * span)
        if stage == len(STAGES) - 1:
            load(sent)
        got = []
        for k, flip in moves:
            pairs = [(i, i ^ flip) for i in range(devices)]
            if forward:
                pairs = [(i, j) for i, j in pairs if i < j]
            got.append((k, lax.ppermute(sent, "ctx", pairs).astype(jnp.float32)))
        total = total * own
        for k, theirs in got:
            other = mine ^ k
            before = before + theirs * power(
                jnp.where(other < mine, (mine - 1 - other) * span + inside, -1)
            )
            total = total + theirs * power((members - 1 - other) * span)
        span *= members
    return before


def on_device(gate_query, gate_key, value_in, residues, decay_rate, skip_gain, out_weight):
    index = lax.axis_index("ctx")
    length, chans = gate_key.shape
    groups = chans // LANES
    ring = lax.axis_size("tp")
    forth = [(i, (i + 1) % ring) for i in range(ring)]
    back = [(i, (i + ring - 1) % ring) for i in range(ring)]

    state, keyed, decay, residue, skip = block_state(
        gate_key, value_in, decay_rate.T, residues.T, skip_gain.reshape(groups, LANES)
    )
    scale = residue * jnp.sqrt(-jnp.expm1(-2.0 * decay))
    local = None

    def work(sent):
        nonlocal local
        local, ahead = local_part(keyed, decay, scale, sent, skip)
        return ahead

    def load(sent):
        nonlocal columns
        columns = fetch(gate_query, out_weight, sent, ring)

    columns = None
    carry = scan_over_ctx(state, decay, length, index, work, load)
    query, far = columns
    start = scale * jnp.exp(-decay) * carry
    gated, far_top, far_low, after = carry_part(local, query, decay, start, far, out_weight)
    far_a = lax.ppermute(far_top, "tp", forth)
    far_b = lax.ppermute(far_low, "tp", back)
    after_top, after_low, prior_top, prior_low = near_part(gated, after, out_weight)
    mine_top, mine_low = own_part(gated, out_weight, ring)
    near_b = lax.ppermute(after_low, "tp", forth)
    near_a = lax.ppermute(prior_top, "tp", back)
    both_a = lax.ppermute((after_top + far_a.astype(jnp.float32)).astype(jnp.bfloat16), "tp", forth)
    both_b = lax.ppermute((prior_low + far_b.astype(jnp.float32)).astype(jnp.bfloat16), "tp", back)
    return finish(mine_top, near_a, both_a, mine_low, near_b, both_b)


def solution(mesh):
    in_specs = (
        P("ctx", "tp"),
        P("ctx", "tp"),
        P("ctx", "tp"),
        P("tp", None),
        P("tp", None),
        P("tp"),
        P("tp", None),
    )
    return jax.shard_map(
        on_device, mesh=mesh, in_specs=in_specs, out_specs=P("ctx", "tp"), check_vma=False
    )
```

```python
import functools

import jax
import jax.numpy as jnp
from jax import lax
from jax.experimental import pallas as pl
from jax.experimental.pallas import tpu as pltpu
from jax.sharding import PartitionSpec as P

MODES = 16
LANES = 128
SUB = 8
ROWS = 16


CHUNKS = 4
CUT = 9
FAR, NEXT, LAST, MINE = 2, 1, 3, 0
STAGES = (
    (2, ((1, 1),), False),
    (4, ((1, 2), (3, 6), (2, 4)), False),
    (4, ((1, 8), (3, 24), (2, 16)), False),
    (2, ((1, 48),), False),
)
WORK = 1
HBM = pl.BlockSpec(memory_space=pltpu.HBM)
VMEM = pl.BlockSpec(memory_space=pltpu.VMEM)
DMA = pltpu.SemaphoreType.DMA


def in_hbm(array):
    return pltpu.with_memory_space_constraint(array, pltpu.HBM)


def params():
    return pltpu.CompilerParams(vmem_limit_bytes=24 * 2**20)


def cost(flops, size):
    return pl.CostEstimate(flops=flops, bytes_accessed=size, transcendentals=0)


def wide(*shape):
    return jax.ShapeDtypeStruct(shape, jnp.float32)


def short(*shape):
    return jax.ShapeDtypeStruct(shape, jnp.bfloat16)


def total_of(terms):
    while len(terms) > 1:
        terms = [sum(terms[j : j + 2]) for j in range(0, len(terms), 2)]
    return terms[0]


def fetch_columns(weight_hbm, turn, out_ref, sems, first=0):
    chans, width = out_ref.shape
    owner = lax.rem(lax.axis_index("tp") + turn, weight_hbm.shape[1] // width)
    columns = pl.ds(pl.multiple_of(owner * width, width), width)
    part = chans // CHUNKS
    copies = []
    for c in range(CHUNKS):
        rows = pl.ds(c * part, part)
        copies.append(
            pltpu.make_async_copy(weight_hbm.at[rows, columns], out_ref.at[rows, :], sems.at[first + c])
        )
        copies[-1].start()
    return copies


def wait_all(copies):
    for copy in copies:
        copy.wait()


def state_kernel(key_hbm, value_hbm, decay_hbm, residue_hbm, skip_hbm,
                 state_ref, keyed_ref, decay_ref, residue_ref, skip_ref,
                 key_buf, value_buf, mode_buf, turn_buf, sems):
    length, chans = key_buf.shape
    groups = chans // LANES
    span = groups * SUB
    part = length // CHUNKS
    small = []
    for n, src in enumerate((decay_hbm, residue_hbm)):
        small.append(pltpu.make_async_copy(src, mode_buf.at[n], sems.at[2 * CHUNKS + n]))
    small[0].start()
    copies = []
    for c in range(CHUNKS):
        rows = pl.ds(c * part, part)
        copies.append((
            pltpu.make_async_copy(key_hbm.at[rows, :], key_buf.at[rows, :], sems.at[2 * c]),
            pltpu.make_async_copy(value_hbm.at[rows, :], value_buf.at[rows, :], sems.at[2 * c + 1]),
        ))
        for copy in copies[-1]:
            copy.start()
    small[1].start()
    skip = pltpu.make_async_copy(skip_hbm, skip_ref, sems.at[2 * CHUNKS + 2])
    skip.start()

    def turn(which, out_ref):
        small[which].wait()
        for m in range(MODES // SUB):
            for g in range(groups):
                turn_buf[(m * groups + g) * SUB : (m * groups + g + 1) * SUB, :] = mode_buf[
                    which, m * SUB : (m + 1) * SUB, g * LANES : (g + 1) * LANES
                ]
        for r in range(MODES):
            out_ref[r] = turn_buf[pl.ds(r // SUB * span + r % SUB, groups, stride=SUB), :]

    turn(0, decay_ref)
    step = [jnp.exp(-decay_ref[r]) for r in range(MODES)]

    def block(i, held):
        rows = pl.ds(pl.multiple_of(i * ROWS, ROWS), ROWS)
        keyed = key_buf[rows, :].astype(jnp.float32) * value_buf[rows, :].astype(jnp.float32)
        for half in range(ROWS // SUB):
            base = (i * (ROWS // SUB) + half) * span
            for g in range(groups):
                keyed_ref[pl.ds(pl.multiple_of(base + g * SUB, SUB), SUB), :] = keyed[
                    half * SUB : (half + 1) * SUB, g * LANES : (g + 1) * LANES
                ]
        for half in range(ROWS // SUB):
            base = (i * (ROWS // SUB) + half) * span
            for s in range(SUB):
                now = keyed_ref[pl.ds(base + s, groups, stride=SUB), :]
                held = [a * h + now for a, h in zip(step, held)]
        return held

    held = [jnp.zeros((groups, LANES), jnp.float32)] * MODES
    for c in range(CHUNKS):
        for copy in copies[c]:
            copy.wait()
        held = lax.fori_loop(c * (part // ROWS), (c + 1) * (part // ROWS), block, held)
    for r in range(MODES):
        state_ref[r] = held[r]
    turn(1, residue_ref)
    skip.wait()


def block_state(gate_key, value_in, decay, residue, skip):
    length, chans = gate_key.shape
    groups = chans // LANES
    modes = wide(MODES, groups, LANES)
    return pl.pallas_call(
        state_kernel,
        out_shape=(modes, wide(length * groups, LANES), modes, modes, wide(groups, LANES)),
        in_specs=[HBM] * 5,
        out_specs=(VMEM,) * 5,
        scratch_shapes=[
            pltpu.VMEM((length, chans), jnp.bfloat16),
            pltpu.VMEM((length, chans), jnp.bfloat16),
            pltpu.VMEM((2, MODES, chans), jnp.float32),
            pltpu.VMEM((MODES * groups, LANES), jnp.float32),
            DMA((2 * CHUNKS + 3,)),
        ],
        compiler_params=params(),
        cost_estimate=cost(2**23, 2**23),
    )(*(in_hbm(x) for x in (gate_key, value_in, decay, residue, skip)))


def local_kernel(members, apart, keyed_ref, decay_ref, scale_ref, _, skip_ref, local_ref, ahead_ref):
    groups = decay_ref.shape[1]
    span = groups * SUB
    ahead = (members - 1 - lax.axis_index("ctx") // apart % members) * apart * (keyed_ref.shape[0] // groups)
    for r in range(MODES):
        ahead_ref[r] = jnp.exp(-decay_ref[r] * ahead.astype(jnp.float32))
    step = [jnp.exp(-decay_ref[r]) for r in range(MODES)]
    scale = [scale_ref[r] for r in range(MODES)]
    skip = skip_ref[...]

    def block(i, held):
        for s in range(SUB):
            at = pl.ds(i * span + s, groups, stride=SUB)
            now = keyed_ref[at, :]
            held = [a * h + now for a, h in zip(step, held)]
            local_ref[at, :] = total_of([c * h for c, h in zip(scale, held)] + [skip * now])
        return held

    lax.fori_loop(0, keyed_ref.shape[0] // span, block, [jnp.zeros((groups, LANES), jnp.float32)] * MODES)


def local_part(members, apart, keyed, decay, scale, behind, skip):
    return pl.pallas_call(
        functools.partial(local_kernel, members, apart),
        out_shape=(wide(*keyed.shape), wide(*decay.shape)),
        in_specs=[VMEM] * 5,
        out_specs=(VMEM, VMEM),
        compiler_params=params(),
        cost_estimate=cost(2**23, 2**22),
    )(keyed, decay, scale, behind, skip)


def apply_gate(mixing, query_ref, gated_ref):
    length, chans = gated_ref.shape
    groups = chans // LANES

    def block(i, _):
        rows = pl.ds(pl.multiple_of(i * ROWS, ROWS), ROWS)
        for g in range(groups):
            cols = slice(g * LANES, (g + 1) * LANES)
            tiles = [mixing(i * (ROWS // SUB) + half, g) for half in range(ROWS // SUB)]
            gated_ref[rows, cols] = (
                query_ref[rows, cols].astype(jnp.float32) * jnp.concatenate(tiles, axis=0)
            ).astype(jnp.bfloat16)
        return 0

    lax.fori_loop(0, length // ROWS, block, 0)


def add_tail(base_ref, decay_ref, start_ref, mix_ref):
    groups = decay_ref.shape[1]
    span = groups * SUB
    step = [jnp.exp(-decay_ref[r]) for r in range(MODES)]

    def block(i, held):
        for s in range(SUB):
            at = pl.ds(i * span + s, groups, stride=SUB)
            mix_ref[at, :] = base_ref[at, :] + total_of(held)
            held = [a * h for a, h in zip(step, held)]
        return held

    lax.fori_loop(0, mix_ref.shape[0] // span, block, [start_ref[r] for r in range(MODES)])


def tile_of(mix_ref, groups):
    def tile(i, g):
        return mix_ref[pl.ds(pl.multiple_of((i * groups + g) * SUB, SUB), SUB), :]

    return tile


def in_upper_half():
    return lax.axis_index("ctx") >= lax.axis_size("ctx") // 2


def begin_kernel(local_ref, decay_ref, start_ref, _, query_hbm, weight_hbm,
                 mix_ref, query_ref, far_ref, next_ref, gated_ref, far_top, far_low, sems):
    upper = in_upper_half()
    query_copy = pltpu.make_async_copy(query_hbm, query_ref, sems.at[CHUNKS])
    query_copy.start()
    far_copies = fetch_columns(weight_hbm, FAR, far_ref, sems)
    next_copies = fetch_columns(weight_hbm, NEXT, next_ref, sems, CHUNKS + 1)
    add_tail(local_ref, decay_ref, start_ref, mix_ref)
    query_copy.wait()

    @pl.when(jnp.logical_not(upper))
    def _():
        apply_gate(tile_of(mix_ref, decay_ref.shape[1]), query_ref, gated_ref)

    wait_all(far_copies)

    @pl.when(jnp.logical_not(upper))
    def _():
        project(gated_ref, far_ref, far_top, far_low)

    wait_all(next_copies)


def begin_part(local, decay, start, behind, gate_query, weight, ring):
    length, chans = gate_query.shape
    width = weight.shape[1] // ring
    columns = short(chans, width)
    top, low = cut_rows(length, width)
    return pl.pallas_call(
        begin_kernel,
        out_shape=(wide(*local.shape), short(length, chans), columns, columns, short(length, chans), short(*top), short(*low)),
        in_specs=[VMEM] * 4 + [HBM] * 2,
        out_specs=(VMEM,) * 7,
        scratch_shapes=[DMA((2 * CHUNKS + 1,))],
        compiler_params=params(),
        cost_estimate=cost(2**23, 2**22),
    )(local, decay, start, behind, in_hbm(gate_query), in_hbm(weight))


def end_kernel(mix_ref, query_ref, far_ref, gated_in, top_in, low_in, decay_ref, start_ref,
               gated_ref, far_top, far_low, sum_ref):
    upper = in_upper_half()

    @pl.when(upper)
    def _():
        add_tail(mix_ref, decay_ref, start_ref, sum_ref)
        apply_gate(tile_of(sum_ref, decay_ref.shape[1]), query_ref, gated_ref)
        project(gated_ref, far_ref, far_top, far_low)

    @pl.when(jnp.logical_not(upper))
    def _():
        for source, out in ((gated_in, gated_ref), (top_in, far_top), (low_in, far_low)):
            out[...] = source[...]


def end_part(begun, decay, start):
    mix, query, far, _, gated, top, low = begun
    return pl.pallas_call(
        end_kernel,
        out_shape=(short(*gated.shape), short(*top.shape), short(*low.shape)),
        in_specs=[VMEM] * 8,
        out_specs=(VMEM,) * 3,
        scratch_shapes=[pltpu.VMEM(mix.shape, jnp.float32)],
        compiler_params=params(),
        cost_estimate=cost(2**29, 2**20),
    )(mix, query, far, gated, top, low, decay, start)


def cut_rows(length, width):
    cut = length * CUT // 16
    return (cut, width), (length - cut, width)


def project(gated_ref, columns_ref, *outs):
    row = 0
    for out in outs:
        rows = slice(row, row + out.shape[0])
        out[...] = jnp.dot(
            gated_ref[rows, :], columns_ref[...], preferred_element_type=jnp.float32
        ).astype(out.dtype)
        row += out.shape[0]


def next_part(gated, columns):
    top, low = cut_rows(gated.shape[0], columns.shape[1])
    return pl.pallas_call(
        project,
        out_shape=(wide(*top), short(*low)),
        in_specs=[VMEM, VMEM],
        out_specs=(VMEM, VMEM),
        compiler_params=params(),
        cost_estimate=cost(2**29, 2**20),
    )(gated, columns)


def fetch_and_project(turn, gated_ref, weight_hbm, _, top_ref, low_ref, columns_ref, sems):
    wait_all(fetch_columns(weight_hbm, turn, columns_ref, sems))
    project(gated_ref, columns_ref, top_ref, low_ref)


def fetched_part(turn, out_shape, gated, weight, behind, ring):
    return pl.pallas_call(
        functools.partial(fetch_and_project, turn),
        out_shape=out_shape,
        in_specs=[VMEM, HBM, VMEM],
        out_specs=(VMEM, VMEM),
        scratch_shapes=[pltpu.VMEM((gated.shape[1], weight.shape[1] // ring), jnp.bfloat16), DMA((CHUNKS,))],
        compiler_params=params(),
        cost_estimate=cost(2**29, 2**21),
    )(gated, in_hbm(weight), behind)


def last_part(gated, weight, behind, ring):
    top, low = cut_rows(gated.shape[0], weight.shape[1] // ring)
    return fetched_part(LAST, (short(*top), wide(*low)), gated, weight, behind, ring)


def own_part(gated, weight, behind, ring):
    top, low = cut_rows(gated.shape[0], weight.shape[1] // ring)
    return fetched_part(MINE, (wide(*top), wide(*low)), gated, weight, behind, ring)


def finish_kernel(mine_top, near_top, both_top, mine_low, near_low, both_low, out_hbm, out_buf, sems):
    row = 0
    copies = []
    for n, (mine, near, both) in enumerate(
        ((mine_top, near_top, both_top), (mine_low, near_low, both_low))
    ):
        rows = pl.ds(row, mine.shape[0])
        out_buf[rows, :] = (
            mine[...] + near[...].astype(jnp.float32) + both[...].astype(jnp.float32)
        ).astype(jnp.bfloat16)
        copies.append(pltpu.make_async_copy(out_buf.at[rows, :], out_hbm.at[rows, :], sems.at[n]))
        copies[-1].start()
        row += mine.shape[0]
    wait_all(copies)


def finish(*parts):
    length, width = parts[0].shape[0] + parts[3].shape[0], parts[0].shape[1]
    return pl.pallas_call(
        finish_kernel,
        out_shape=short(length, width),
        in_specs=[VMEM] * 6,
        out_specs=HBM,
        scratch_shapes=[pltpu.VMEM((length, width), jnp.bfloat16), DMA((2,))],
        compiler_params=params(),
        cost_estimate=cost(2**19, 2**21),
    )(*parts)


def scan_over_ctx(state, decay, length, index, work, load):
    devices = lax.axis_size("ctx")

    def power(blocks):
        blocks = jnp.asarray(blocks)
        reach = (length * jnp.maximum(blocks, 0)).astype(jnp.float32)
        return jnp.where(blocks >= 0, jnp.exp(-decay * reach), 0.0)

    total, before = state, jnp.zeros_like(state)
    span = 1
    for stage, (members, moves, forward) in enumerate(STAGES):
        mine, inside = index // span % members, index % span
        sent = total.astype(jnp.bfloat16)
        own = work(sent, members, span) if stage == WORK else power((members - 1 - mine) * span)
        if stage == len(STAGES) - 1:
            load(sent, before)
            before = jnp.zeros_like(state)
        got = []
        for k, flip in moves:
            pairs = [(i, i ^ flip) for i in range(devices)]
            if forward:
                pairs = [(i, j) for i, j in pairs if i < j]
            got.append((k, lax.ppermute(sent, "ctx", pairs).astype(jnp.float32)))
        total = total * own
        for k, theirs in got:
            other = mine ^ k
            before = before + theirs * power(
                jnp.where(other < mine, (mine - 1 - other) * span + inside, -1)
            )
            total = total + theirs * power((members - 1 - other) * span)
        span *= members
    return before


def on_device(gate_query, gate_key, value_in, residues, decay_rate, skip_gain, out_weight):
    index = lax.axis_index("ctx")
    length, chans = gate_key.shape
    groups = chans // LANES
    ring = lax.axis_size("tp")
    forth = [(i, (i + NEXT) % ring) for i in range(ring)]
    back = [(i, (i + LAST) % ring) for i in range(ring)]

    state, keyed, decay, residue, skip = block_state(
        gate_key, value_in, decay_rate.T, residues.T, skip_gain.reshape(groups, LANES)
    )
    scale = residue * jnp.sqrt(-jnp.expm1(-2.0 * decay))
    local = None

    def work(sent, members, apart):
        nonlocal local
        local, ahead = local_part(members, apart, keyed, decay, scale, sent, skip)
        return ahead

    entry = scale * jnp.exp(-decay)

    def load(sent, before):
        nonlocal begun
        begun = begin_part(local, decay, entry * before, sent, gate_query, out_weight, ring)

    begun = None
    carry = scan_over_ctx(state, decay, length, index, work, load)
    gated, far_top, far_low = end_part(begun, decay, entry * carry)
    far_a = lax.ppermute(far_top, "tp", forth)
    far_b = lax.ppermute(far_low, "tp", back)
    next_top, next_low = next_part(gated, begun[3])
    near_b = lax.ppermute(next_low, "tp", forth)
    last_top, last_low = last_part(gated, out_weight, next_low, ring)
    near_a = lax.ppermute(last_top, "tp", back)
    mine_top, mine_low = own_part(gated, out_weight, last_top, ring)
    both_a = lax.ppermute((next_top + far_a.astype(jnp.float32)).astype(jnp.bfloat16), "tp", forth)
    both_b = lax.ppermute((last_low + far_b.astype(jnp.float32)).astype(jnp.bfloat16), "tp", back)
    return finish(mine_top, near_a, both_a, mine_low, near_b, both_b)


def solution(mesh):
    in_specs = (
        P("ctx", "tp"),
        P("ctx", "tp"),
        P("ctx", "tp"),
        P("tp", None),
        P("tp", None),
        P("tp"),
        P("tp", None),
    )
    return jax.shard_map(
        on_device, mesh=mesh, in_specs=in_specs, out_specs=P("ctx", "tp"), check_vma=False
    )
```

```python
import functools

import jax
import jax.numpy as jnp
from jax import lax
from jax.experimental import pallas as pl
from jax.experimental.pallas import tpu as pltpu
from jax.sharding import PartitionSpec as P

MODES = 16
LANES = 128
SUB = 8
ROWS = 16


CHUNKS = 4
CUT = 9
FAR, NEXT, LAST, MINE = 2, 1, 3, 0
STAGES = (
    (2, ((1, 1),), False),
    (4, ((1, 2), (3, 6), (2, 4)), False),
    (4, ((1, 8), (3, 24), (2, 16)), False),
    (2, ((1, 48),), False),
)
WORK = (1, 2)
HBM = pl.BlockSpec(memory_space=pltpu.HBM)
VMEM = pl.BlockSpec(memory_space=pltpu.VMEM)
DMA = pltpu.SemaphoreType.DMA


def in_hbm(array):
    return pltpu.with_memory_space_constraint(array, pltpu.HBM)


def params():
    return pltpu.CompilerParams(vmem_limit_bytes=24 * 2**20)


def cost(flops, size):
    return pl.CostEstimate(flops=flops, bytes_accessed=size, transcendentals=0)


def wide(*shape):
    return jax.ShapeDtypeStruct(shape, jnp.float32)


def short(*shape):
    return jax.ShapeDtypeStruct(shape, jnp.bfloat16)


def total_of(terms):
    while len(terms) > 1:
        terms = [sum(terms[j : j + 2]) for j in range(0, len(terms), 2)]
    return terms[0]


def fetch_columns(weight_hbm, turn, out_ref, sems, first=0):
    chans, width = out_ref.shape
    owner = lax.rem(lax.axis_index("tp") + turn, weight_hbm.shape[1] // width)
    columns = pl.ds(pl.multiple_of(owner * width, width), width)
    part = chans // CHUNKS
    copies = []
    for c in range(CHUNKS):
        rows = pl.ds(c * part, part)
        copies.append(
            pltpu.make_async_copy(weight_hbm.at[rows, columns], out_ref.at[rows, :], sems.at[first + c])
        )
        copies[-1].start()
    return copies


def wait_all(copies):
    for copy in copies:
        copy.wait()


def state_kernel(key_hbm, value_hbm, decay_hbm, residue_hbm, skip_hbm,
                 state_ref, keyed_ref, decay_ref, residue_ref, skip_ref,
                 key_buf, value_buf, mode_buf, turn_buf, sems):
    length, chans = key_buf.shape
    groups = chans // LANES
    span = groups * SUB
    part = length // CHUNKS
    small = []
    for n, src in enumerate((decay_hbm, residue_hbm)):
        small.append(pltpu.make_async_copy(src, mode_buf.at[n], sems.at[2 * CHUNKS + n]))
    small[0].start()
    copies = []
    for c in range(CHUNKS):
        rows = pl.ds(c * part, part)
        copies.append((
            pltpu.make_async_copy(key_hbm.at[rows, :], key_buf.at[rows, :], sems.at[2 * c]),
            pltpu.make_async_copy(value_hbm.at[rows, :], value_buf.at[rows, :], sems.at[2 * c + 1]),
        ))
        for copy in copies[-1]:
            copy.start()
    small[1].start()
    skip = pltpu.make_async_copy(skip_hbm, skip_ref, sems.at[2 * CHUNKS + 2])
    skip.start()

    def turn(which, out_ref):
        small[which].wait()
        for m in range(MODES // SUB):
            for g in range(groups):
                turn_buf[(m * groups + g) * SUB : (m * groups + g + 1) * SUB, :] = mode_buf[
                    which, m * SUB : (m + 1) * SUB, g * LANES : (g + 1) * LANES
                ]
        for r in range(MODES):
            out_ref[r] = turn_buf[pl.ds(r // SUB * span + r % SUB, groups, stride=SUB), :]

    turn(0, decay_ref)
    step = [jnp.exp(-decay_ref[r]) for r in range(MODES)]

    def block(i, held):
        rows = pl.ds(pl.multiple_of(i * ROWS, ROWS), ROWS)
        keyed = key_buf[rows, :].astype(jnp.float32) * value_buf[rows, :].astype(jnp.float32)
        for half in range(ROWS // SUB):
            base = (i * (ROWS // SUB) + half) * span
            for g in range(groups):
                keyed_ref[pl.ds(pl.multiple_of(base + g * SUB, SUB), SUB), :] = keyed[
                    half * SUB : (half + 1) * SUB, g * LANES : (g + 1) * LANES
                ]
        for half in range(ROWS // SUB):
            base = (i * (ROWS // SUB) + half) * span
            for s in range(SUB):
                now = keyed_ref[pl.ds(base + s, groups, stride=SUB), :]
                held = [a * h + now for a, h in zip(step, held)]
        return held

    held = [jnp.zeros((groups, LANES), jnp.float32)] * MODES
    for c in range(CHUNKS):
        for copy in copies[c]:
            copy.wait()
        held = lax.fori_loop(c * (part // ROWS), (c + 1) * (part // ROWS), block, held)
    for r in range(MODES):
        state_ref[r] = held[r]
    turn(1, residue_ref)
    skip.wait()


def block_state(gate_key, value_in, decay, residue, skip):
    length, chans = gate_key.shape
    groups = chans // LANES
    modes = wide(MODES, groups, LANES)
    return pl.pallas_call(
        state_kernel,
        out_shape=(modes, wide(length * groups, LANES), modes, modes, wide(groups, LANES)),
        in_specs=[HBM] * 5,
        out_specs=(VMEM,) * 5,
        scratch_shapes=[
            pltpu.VMEM((length, chans), jnp.bfloat16),
            pltpu.VMEM((length, chans), jnp.bfloat16),
            pltpu.VMEM((2, MODES, chans), jnp.float32),
            pltpu.VMEM((MODES * groups, LANES), jnp.float32),
            DMA((2 * CHUNKS + 3,)),
        ],
        compiler_params=params(),
        cost_estimate=cost(2**23, 2**23),
    )(*(in_hbm(x) for x in (gate_key, value_in, decay, residue, skip)))


def local_kernel(part, members, apart, keyed_ref, decay_ref, scale_ref, held_ref, _, skip_ref,
                 local_ref, ahead_ref, left_ref=None):
    groups = decay_ref.shape[1]
    span = groups * SUB
    first = part * local_ref.shape[0]
    ahead = (members - 1 - lax.axis_index("ctx") // apart % members) * apart * (keyed_ref.shape[0] // groups)
    for r in range(MODES):
        ahead_ref[r] = jnp.exp(-decay_ref[r] * ahead.astype(jnp.float32))
    step = [jnp.exp(-decay_ref[r]) for r in range(MODES)]
    scale = [scale_ref[r] for r in range(MODES)]
    skip = skip_ref[...]

    def block(i, held):
        for s in range(SUB):
            now = keyed_ref[pl.ds(first + i * span + s, groups, stride=SUB), :]
            held = [a * h + now for a, h in zip(step, held)]
            local_ref[pl.ds(i * span + s, groups, stride=SUB), :] = total_of(
                [c * h for c, h in zip(scale, held)] + [skip * now]
            )
        return held

    if part:
        held = [held_ref[r] for r in range(MODES)]
    else:
        held = [jnp.zeros((groups, LANES), jnp.float32)] * MODES
    held = lax.fori_loop(0, local_ref.shape[0] // span, block, held)
    if left_ref is not None:
        for r in range(MODES):
            left_ref[r] = held[r]


def local_part(part, members, apart, keyed, decay, scale, held, behind, skip):
    return pl.pallas_call(
        functools.partial(local_kernel, part, members, apart),
        out_shape=(wide(keyed.shape[0] // 2, LANES),) + (wide(*decay.shape),) * (2 - part),
        in_specs=[VMEM] * 6,
        out_specs=(VMEM,) * (3 - part),
        compiler_params=params(),
        cost_estimate=cost(2**22, 2**21),
    )(keyed, decay, scale, held, behind, skip)


def apply_gate(mixing, query_ref, gated_ref):
    length, chans = gated_ref.shape
    groups = chans // LANES

    def block(i, _):
        rows = pl.ds(pl.multiple_of(i * ROWS, ROWS), ROWS)
        for g in range(groups):
            cols = slice(g * LANES, (g + 1) * LANES)
            tiles = [mixing(i * (ROWS // SUB) + half, g) for half in range(ROWS // SUB)]
            gated_ref[rows, cols] = (
                query_ref[rows, cols].astype(jnp.float32) * jnp.concatenate(tiles, axis=0)
            ).astype(jnp.bfloat16)
        return 0

    lax.fori_loop(0, length // ROWS, block, 0)


def add_tail(bases, decay_ref, start_ref, mix_ref):
    groups = decay_ref.shape[1]
    span = groups * SUB
    step = [jnp.exp(-decay_ref[r]) for r in range(MODES)]

    held = [start_ref[r] for r in range(MODES)]
    first = 0
    for base_ref in bases:

        def block(i, held, base_ref=base_ref, first=first):
            for s in range(SUB):
                mix_ref[pl.ds(first + i * span + s, groups, stride=SUB), :] = base_ref[
                    pl.ds(i * span + s, groups, stride=SUB), :
                ] + total_of(held)
                held = [a * h for a, h in zip(step, held)]
            return held

        held = lax.fori_loop(0, base_ref.shape[0] // span, block, held)
        first += base_ref.shape[0]


def tile_of(mix_ref, groups):
    def tile(i, g):
        return mix_ref[pl.ds(pl.multiple_of((i * groups + g) * SUB, SUB), SUB), :]

    return tile


def in_upper_half():
    return lax.axis_index("ctx") >= lax.axis_size("ctx") // 2


def begin_kernel(early_ref, late_ref, decay_ref, start_ref, _, query_hbm, weight_hbm,
                 mix_ref, query_ref, far_ref, next_ref, gated_ref, far_top, far_low, sems):
    upper = in_upper_half()
    query_copy = pltpu.make_async_copy(query_hbm, query_ref, sems.at[CHUNKS])
    query_copy.start()
    far_copies = fetch_columns(weight_hbm, FAR, far_ref, sems)
    next_copies = fetch_columns(weight_hbm, NEXT, next_ref, sems, CHUNKS + 1)
    add_tail((early_ref, late_ref), decay_ref, start_ref, mix_ref)
    query_copy.wait()

    @pl.when(jnp.logical_not(upper))
    def _():
        apply_gate(tile_of(mix_ref, decay_ref.shape[1]), query_ref, gated_ref)

    wait_all(far_copies)

    @pl.when(jnp.logical_not(upper))
    def _():
        project(gated_ref, far_ref, far_top, far_low)

    wait_all(next_copies)


def begin_part(local, decay, start, behind, gate_query, weight, ring):
    length, chans = gate_query.shape
    width = weight.shape[1] // ring
    columns = short(chans, width)
    top, low = cut_rows(length, width)
    return pl.pallas_call(
        begin_kernel,
        out_shape=(wide(2 * local[0].shape[0], LANES), short(length, chans), columns, columns, short(length, chans), short(*top), short(*low)),
        in_specs=[VMEM] * 5 + [HBM] * 2,
        out_specs=(VMEM,) * 7,
        scratch_shapes=[DMA((2 * CHUNKS + 1,))],
        compiler_params=params(),
        cost_estimate=cost(2**23, 2**22),
    )(*local, decay, start, behind, in_hbm(gate_query), in_hbm(weight))


def end_kernel(mix_ref, query_ref, far_ref, gated_in, top_in, low_in, decay_ref, start_ref,
               gated_ref, far_top, far_low, sum_ref):
    upper = in_upper_half()

    @pl.when(upper)
    def _():
        add_tail((mix_ref,), decay_ref, start_ref, sum_ref)
        apply_gate(tile_of(sum_ref, decay_ref.shape[1]), query_ref, gated_ref)
        project(gated_ref, far_ref, far_top, far_low)

    @pl.when(jnp.logical_not(upper))
    def _():
        for source, out in ((gated_in, gated_ref), (top_in, far_top), (low_in, far_low)):
            out[...] = source[...]


def end_part(begun, decay, start):
    mix, query, far, _, gated, top, low = begun
    return pl.pallas_call(
        end_kernel,
        out_shape=(short(*gated.shape), short(*top.shape), short(*low.shape)),
        in_specs=[VMEM] * 8,
        out_specs=(VMEM,) * 3,
        scratch_shapes=[pltpu.VMEM(mix.shape, jnp.float32)],
        compiler_params=params(),
        cost_estimate=cost(2**29, 2**20),
    )(mix, query, far, gated, top, low, decay, start)


def cut_rows(length, width):
    cut = length * CUT // 16
    return (cut, width), (length - cut, width)


def project(gated_ref, columns_ref, *outs):
    row = 0
    for out in outs:
        rows = slice(row, row + out.shape[0])
        out[...] = jnp.dot(
            gated_ref[rows, :], columns_ref[...], preferred_element_type=jnp.float32
        ).astype(out.dtype)
        row += out.shape[0]


def next_part(gated, columns):
    top, low = cut_rows(gated.shape[0], columns.shape[1])
    return pl.pallas_call(
        project,
        out_shape=(wide(*top), short(*low)),
        in_specs=[VMEM, VMEM],
        out_specs=(VMEM, VMEM),
        compiler_params=params(),
        cost_estimate=cost(2**29, 2**20),
    )(gated, columns)


def fetch_and_project(turn, gated_ref, weight_hbm, _, top_ref, low_ref, columns_ref, sems):
    wait_all(fetch_columns(weight_hbm, turn, columns_ref, sems))
    project(gated_ref, columns_ref, top_ref, low_ref)


def fetched_part(turn, out_shape, gated, weight, behind, ring):
    return pl.pallas_call(
        functools.partial(fetch_and_project, turn),
        out_shape=out_shape,
        in_specs=[VMEM, HBM, VMEM],
        out_specs=(VMEM, VMEM),
        scratch_shapes=[pltpu.VMEM((gated.shape[1], weight.shape[1] // ring), jnp.bfloat16), DMA((CHUNKS,))],
        compiler_params=params(),
        cost_estimate=cost(2**29, 2**21),
    )(gated, in_hbm(weight), behind)


def last_part(gated, weight, behind, ring):
    top, low = cut_rows(gated.shape[0], weight.shape[1] // ring)
    return fetched_part(LAST, (short(*top), wide(*low)), gated, weight, behind, ring)


def own_part(gated, weight, behind, ring):
    top, low = cut_rows(gated.shape[0], weight.shape[1] // ring)
    return fetched_part(MINE, (wide(*top), wide(*low)), gated, weight, behind, ring)


def finish_kernel(mine_top, near_top, both_top, mine_low, near_low, both_low, out_hbm, out_buf, sems):
    row = 0
    copies = []
    for n, (mine, near, both) in enumerate(
        ((mine_top, near_top, both_top), (mine_low, near_low, both_low))
    ):
        rows = pl.ds(row, mine.shape[0])
        out_buf[rows, :] = (
            mine[...] + near[...].astype(jnp.float32) + both[...].astype(jnp.float32)
        ).astype(jnp.bfloat16)
        copies.append(pltpu.make_async_copy(out_buf.at[rows, :], out_hbm.at[rows, :], sems.at[n]))
        copies[-1].start()
        row += mine.shape[0]
    wait_all(copies)


def finish(*parts):
    length, width = parts[0].shape[0] + parts[3].shape[0], parts[0].shape[1]
    return pl.pallas_call(
        finish_kernel,
        out_shape=short(length, width),
        in_specs=[VMEM] * 6,
        out_specs=HBM,
        scratch_shapes=[pltpu.VMEM((length, width), jnp.bfloat16), DMA((2,))],
        compiler_params=params(),
        cost_estimate=cost(2**19, 2**21),
    )(*parts)


def scan_over_ctx(state, decay, length, index, work, load):
    devices = lax.axis_size("ctx")

    def power(blocks):
        blocks = jnp.asarray(blocks)
        reach = (length * jnp.maximum(blocks, 0)).astype(jnp.float32)
        return jnp.where(blocks >= 0, jnp.exp(-decay * reach), 0.0)

    total, before = state, jnp.zeros_like(state)
    span = 1
    for stage, (members, moves, forward) in enumerate(STAGES):
        mine, inside = index // span % members, index % span
        sent = total.astype(jnp.bfloat16)
        own = work(sent, members, span) if stage in WORK else power((members - 1 - mine) * span)
        if stage == len(STAGES) - 1:
            load(sent, before)
            before = jnp.zeros_like(state)
        got = []
        for k, flip in moves:
            pairs = [(i, i ^ flip) for i in range(devices)]
            if forward:
                pairs = [(i, j) for i, j in pairs if i < j]
            got.append((k, lax.ppermute(sent, "ctx", pairs).astype(jnp.float32)))
        total = total * own
        for k, theirs in got:
            other = mine ^ k
            before = before + theirs * power(
                jnp.where(other < mine, (mine - 1 - other) * span + inside, -1)
            )
            total = total + theirs * power((members - 1 - other) * span)
        span *= members
    return before


def on_device(gate_query, gate_key, value_in, residues, decay_rate, skip_gain, out_weight):
    index = lax.axis_index("ctx")
    length, chans = gate_key.shape
    groups = chans // LANES
    ring = lax.axis_size("tp")
    forth = [(i, (i + NEXT) % ring) for i in range(ring)]
    back = [(i, (i + LAST) % ring) for i in range(ring)]

    state, keyed, decay, residue, skip = block_state(
        gate_key, value_in, decay_rate.T, residues.T, skip_gain.reshape(groups, LANES)
    )
    scale = residue * jnp.sqrt(-jnp.expm1(-2.0 * decay))
    local, held = [], state

    def work(sent, members, apart):
        nonlocal held
        part, ahead, *left = local_part(len(local), members, apart, keyed, decay, scale, held, sent, skip)
        local.append(part)
        held = left[0] if left else held
        return ahead

    entry = scale * jnp.exp(-decay)

    def load(sent, before):
        nonlocal begun
        begun = begin_part(local, decay, entry * before, sent, gate_query, out_weight, ring)

    begun = None
    carry = scan_over_ctx(state, decay, length, index, work, load)
    gated, far_top, far_low = end_part(begun, decay, entry * carry)
    far_a = lax.ppermute(far_top, "tp", forth)
    far_b = lax.ppermute(far_low, "tp", back)
    next_top, next_low = next_part(gated, begun[3])
    near_b = lax.ppermute(next_low, "tp", forth)
    last_top, last_low = last_part(gated, out_weight, next_low, ring)
    near_a = lax.ppermute(last_top, "tp", back)
    mine_top, mine_low = own_part(gated, out_weight, last_top, ring)
    both_a = lax.ppermute((next_top + far_a.astype(jnp.float32)).astype(jnp.bfloat16), "tp", forth)
    both_b = lax.ppermute((last_low + far_b.astype(jnp.float32)).astype(jnp.bfloat16), "tp", back)
    return finish(mine_top, near_a, both_a, mine_low, near_b, both_b)


def solution(mesh):
    in_specs = (
        P("ctx", "tp"),
        P("ctx", "tp"),
        P("ctx", "tp"),
        P("tp", None),
        P("tp", None),
        P("tp"),
        P("tp", None),
    )
    return jax.shard_map(
        on_device, mesh=mesh, in_specs=in_specs, out_specs=P("ctx", "tp"), check_vma=False
    )
```

```python
import functools

import jax
import jax.numpy as jnp
from jax import lax
from jax.experimental import pallas as pl
from jax.experimental.pallas import tpu as pltpu
from jax.sharding import PartitionSpec as P

MODES = 16
LANES = 128
SUB = 8
ROWS = 16


CHUNKS = 4
CUT = 9
FAR, NEXT, LAST, MINE = 2, 1, 3, 0
STAGES = (
    (2, ((1, 1),), False),
    (4, ((1, 2), (3, 6), (2, 4)), False),
    (4, ((1, 8), (3, 24), (2, 16)), False),
    (2, ((1, 48),), False),
)
WORK = (1, 2)
HBM = pl.BlockSpec(memory_space=pltpu.HBM)
VMEM = pl.BlockSpec(memory_space=pltpu.VMEM)
DMA = pltpu.SemaphoreType.DMA


def in_hbm(array):
    return pltpu.with_memory_space_constraint(array, pltpu.HBM)


def params():
    return pltpu.CompilerParams(vmem_limit_bytes=24 * 2**20)


def cost(flops, size):
    return pl.CostEstimate(flops=flops, bytes_accessed=size, transcendentals=0)


def wide(*shape):
    return jax.ShapeDtypeStruct(shape, jnp.float32)


def short(*shape):
    return jax.ShapeDtypeStruct(shape, jnp.bfloat16)


def total_of(terms):
    while len(terms) > 1:
        terms = [sum(terms[j : j + 2]) for j in range(0, len(terms), 2)]
    return terms[0]


def fetch_columns(weight_hbm, turn, out_ref, sems, first=0):
    chans, width = out_ref.shape
    owner = lax.rem(lax.axis_index("tp") + turn, weight_hbm.shape[1] // width)
    columns = pl.ds(pl.multiple_of(owner * width, width), width)
    part = chans // CHUNKS
    copies = []
    for c in range(CHUNKS):
        rows = pl.ds(c * part, part)
        copies.append(
            pltpu.make_async_copy(weight_hbm.at[rows, columns], out_ref.at[rows, :], sems.at[first + c])
        )
        copies[-1].start()
    return copies


def wait_all(copies):
    for copy in copies:
        copy.wait()


def state_kernel(key_hbm, value_hbm, decay_hbm, residue_hbm, skip_hbm,
                 state_ref, keyed_ref, decay_ref, residue_ref, skip_ref,
                 key_buf, value_buf, mode_buf, turn_buf, sems):
    length, chans = key_buf.shape
    groups = chans // LANES
    span = groups * SUB
    part = length // CHUNKS
    small = []
    for n, src in enumerate((decay_hbm, residue_hbm)):
        small.append(pltpu.make_async_copy(src, mode_buf.at[n], sems.at[2 * CHUNKS + n]))
    small[0].start()
    copies = []
    for c in range(CHUNKS):
        rows = pl.ds(c * part, part)
        copies.append((
            pltpu.make_async_copy(key_hbm.at[rows, :], key_buf.at[rows, :], sems.at[2 * c]),
            pltpu.make_async_copy(value_hbm.at[rows, :], value_buf.at[rows, :], sems.at[2 * c + 1]),
        ))
        for copy in copies[-1]:
            copy.start()
    small[1].start()
    skip = pltpu.make_async_copy(skip_hbm, skip_ref, sems.at[2 * CHUNKS + 2])
    skip.start()

    def turn(which, out_ref):
        small[which].wait()
        for m in range(MODES // SUB):
            for g in range(groups):
                turn_buf[(m * groups + g) * SUB : (m * groups + g + 1) * SUB, :] = mode_buf[
                    which, m * SUB : (m + 1) * SUB, g * LANES : (g + 1) * LANES
                ]
        for r in range(MODES):
            out_ref[r] = turn_buf[pl.ds(r // SUB * span + r % SUB, groups, stride=SUB), :]

    turn(0, decay_ref)
    step = [jnp.exp(-decay_ref[r]) for r in range(MODES)]

    def block(i, held):
        rows = pl.ds(pl.multiple_of(i * ROWS, ROWS), ROWS)
        keyed = (key_buf[rows, :] * value_buf[rows, :]).astype(jnp.float32)
        for half in range(ROWS // SUB):
            base = (i * (ROWS // SUB) + half) * span
            for g in range(groups):
                keyed_ref[pl.ds(pl.multiple_of(base + g * SUB, SUB), SUB), :] = keyed[
                    half * SUB : (half + 1) * SUB, g * LANES : (g + 1) * LANES
                ]
        for half in range(ROWS // SUB):
            base = (i * (ROWS // SUB) + half) * span
            for s in range(SUB):
                now = keyed_ref[pl.ds(base + s, groups, stride=SUB), :]
                held = [a * h + now for a, h in zip(step, held)]
        return held

    held = [jnp.zeros((groups, LANES), jnp.float32)] * MODES
    for c in range(CHUNKS):
        for copy in copies[c]:
            copy.wait()
        held = lax.fori_loop(c * (part // ROWS), (c + 1) * (part // ROWS), block, held)
    for r in range(MODES):
        state_ref[r] = held[r]
    turn(1, residue_ref)
    skip.wait()


def block_state(gate_key, value_in, decay, residue, skip):
    length, chans = gate_key.shape
    groups = chans // LANES
    modes = wide(MODES, groups, LANES)
    return pl.pallas_call(
        state_kernel,
        out_shape=(modes, wide(length * groups, LANES), modes, modes, wide(groups, LANES)),
        in_specs=[HBM] * 5,
        out_specs=(VMEM,) * 5,
        scratch_shapes=[
            pltpu.VMEM((length, chans), jnp.bfloat16),
            pltpu.VMEM((length, chans), jnp.bfloat16),
            pltpu.VMEM((2, MODES, chans), jnp.float32),
            pltpu.VMEM((MODES * groups, LANES), jnp.float32),
            DMA((2 * CHUNKS + 3,)),
        ],
        compiler_params=params(),
        cost_estimate=cost(2**23, 2**23),
    )(*(in_hbm(x) for x in (gate_key, value_in, decay, residue, skip)))


def local_kernel(part, members, apart, keyed_ref, decay_ref, scale_ref, held_ref, _, skip_ref,
                 local_ref, ahead_ref, left_ref=None):
    groups = decay_ref.shape[1]
    span = groups * SUB
    first = part * local_ref.shape[0]
    ahead = (members - 1 - lax.axis_index("ctx") // apart % members) * apart * (keyed_ref.shape[0] // groups)
    for r in range(MODES):
        ahead_ref[r] = jnp.exp(-decay_ref[r] * ahead.astype(jnp.float32))
    step = [jnp.exp(-decay_ref[r]) for r in range(MODES)]
    scale = [scale_ref[r] for r in range(MODES)]
    skip = skip_ref[...]

    def block(i, held):
        for s in range(SUB):
            now = keyed_ref[pl.ds(first + i * span + s, groups, stride=SUB), :]
            held = [a * h + now for a, h in zip(step, held)]
            local_ref[pl.ds(i * span + s, groups, stride=SUB), :] = total_of(
                [c * h for c, h in zip(scale, held)] + [skip * now]
            )
        return held

    if part:
        held = [held_ref[r] for r in range(MODES)]
    else:
        held = [jnp.zeros((groups, LANES), jnp.float32)] * MODES
    held = lax.fori_loop(0, local_ref.shape[0] // span, block, held)
    if left_ref is not None:
        for r in range(MODES):
            left_ref[r] = held[r]


def local_part(part, members, apart, keyed, decay, scale, held, behind, skip):
    return pl.pallas_call(
        functools.partial(local_kernel, part, members, apart),
        out_shape=(wide(keyed.shape[0] // 2, LANES),) + (wide(*decay.shape),) * (2 - part),
        in_specs=[VMEM] * 6,
        out_specs=(VMEM,) * (3 - part),
        compiler_params=params(),
        cost_estimate=cost(2**22, 2**21),
    )(keyed, decay, scale, held, behind, skip)


def apply_gate(mixing, query_ref, gated_ref):
    length, chans = gated_ref.shape
    groups = chans // LANES

    def block(i, _):
        rows = pl.ds(pl.multiple_of(i * ROWS, ROWS), ROWS)
        for g in range(groups):
            cols = slice(g * LANES, (g + 1) * LANES)
            tiles = [mixing(i * (ROWS // SUB) + half, g) for half in range(ROWS // SUB)]
            gated_ref[rows, cols] = (
                query_ref[rows, cols].astype(jnp.float32) * jnp.concatenate(tiles, axis=0)
            ).astype(jnp.bfloat16)
        return 0

    lax.fori_loop(0, length // ROWS, block, 0)


def add_tail(bases, decay_ref, start_ref, mix_ref):
    groups = decay_ref.shape[1]
    span = groups * SUB
    step = [jnp.exp(-decay_ref[r]) for r in range(MODES)]

    held = [start_ref[r] for r in range(MODES)]
    first = 0
    for base_ref in bases:

        def block(i, held, base_ref=base_ref, first=first):
            for s in range(SUB):
                mix_ref[pl.ds(first + i * span + s, groups, stride=SUB), :] = base_ref[
                    pl.ds(i * span + s, groups, stride=SUB), :
                ] + total_of(held)
                held = [a * h for a, h in zip(step, held)]
            return held

        held = lax.fori_loop(0, base_ref.shape[0] // span, block, held)
        first += base_ref.shape[0]


def tile_of(mix_ref, groups):
    def tile(i, g):
        return mix_ref[pl.ds(pl.multiple_of((i * groups + g) * SUB, SUB), SUB), :]

    return tile


def in_upper_half():
    return lax.axis_index("ctx") >= lax.axis_size("ctx") // 2


def begin_kernel(early_ref, late_ref, decay_ref, start_ref, _, query_hbm, weight_hbm,
                 mix_ref, query_ref, far_ref, next_ref, gated_ref, far_top, far_low, sems):
    upper = in_upper_half()
    query_copy = pltpu.make_async_copy(query_hbm, query_ref, sems.at[CHUNKS])
    query_copy.start()
    far_copies = fetch_columns(weight_hbm, FAR, far_ref, sems)
    next_copies = fetch_columns(weight_hbm, NEXT, next_ref, sems, CHUNKS + 1)
    add_tail((early_ref, late_ref), decay_ref, start_ref, mix_ref)
    query_copy.wait()

    @pl.when(jnp.logical_not(upper))
    def _():
        apply_gate(tile_of(mix_ref, decay_ref.shape[1]), query_ref, gated_ref)

    wait_all(far_copies)

    @pl.when(jnp.logical_not(upper))
    def _():
        project(gated_ref, far_ref, far_top, far_low)

    wait_all(next_copies)


def begin_part(local, decay, start, behind, gate_query, weight, ring):
    length, chans = gate_query.shape
    width = weight.shape[1] // ring
    columns = short(chans, width)
    top, low = cut_rows(length, width)
    return pl.pallas_call(
        begin_kernel,
        out_shape=(wide(2 * local[0].shape[0], LANES), short(length, chans), columns, columns, short(length, chans), short(*top), short(*low)),
        in_specs=[VMEM] * 5 + [HBM] * 2,
        out_specs=(VMEM,) * 7,
        scratch_shapes=[DMA((2 * CHUNKS + 1,))],
        compiler_params=params(),
        cost_estimate=cost(2**23, 2**22),
    )(*local, decay, start, behind, in_hbm(gate_query), in_hbm(weight))


def carry_gate_project(bases, decay_ref, start_ref, mix_ref, query_ref, far_ref, gated_ref, far_top, far_low):
    groups = decay_ref.shape[1]
    span = groups * SUB
    cut = far_top.shape[0]
    step = [jnp.exp(-decay_ref[r]) for r in range(MODES)]
    tile = tile_of(mix_ref, groups)

    def advance(base_ref, first, i, held):
        for s in range(SUB):
            mix_ref[pl.ds(first + i * span + s, groups, stride=SUB), :] = base_ref[
                pl.ds(i * span + s, groups, stride=SUB), :
            ] + total_of(held)
            held = [a * h for a, h in zip(step, held)]
        return held

    def gate(i):
        rows = pl.ds(i * ROWS, ROWS)
        for g in range(groups):
            cols = slice(g * LANES, (g + 1) * LANES)
            tiles = [tile(i * (ROWS // SUB) + half, g) for half in range(ROWS // SUB)]
            gated_ref[rows, cols] = (
                query_ref[rows, cols].astype(jnp.float32) * jnp.concatenate(tiles, axis=0)
            ).astype(jnp.bfloat16)

    held = [start_ref[r] for r in range(MODES)]
    first, done, rest = 0, 0, []
    for base_ref in bases:
        blocks = base_ref.shape[0] // span
        top = min(blocks, cut // SUB - done)
        held = lax.fori_loop(0, top, functools.partial(advance, base_ref, first), held)
        rest += [(base_ref, first, i) for i in range(top, blocks)]
        first += base_ref.shape[0]
        done += top
    lax.fori_loop(0, cut // ROWS, lambda i, _: (gate(i), 0)[1], 0)
    far_top[...] = jnp.dot(gated_ref[:cut, :], far_ref[...], preferred_element_type=jnp.float32).astype(jnp.bfloat16)
    for base_ref, first, i in rest:
        held = advance(base_ref, first, i, held)
    for i in range(cut // ROWS, gated_ref.shape[0] // ROWS):
        gate(i)
    far_low[...] = jnp.dot(gated_ref[cut:, :], far_ref[...], preferred_element_type=jnp.float32).astype(jnp.bfloat16)


def end_kernel(mix_ref, query_ref, far_ref, gated_in, top_in, low_in, decay_ref, start_ref,
               gated_ref, far_top, far_low, sum_ref):
    upper = in_upper_half()

    @pl.when(upper)
    def _():
        carry_gate_project((mix_ref,), decay_ref, start_ref, sum_ref, query_ref, far_ref, gated_ref, far_top, far_low)

    @pl.when(jnp.logical_not(upper))
    def _():
        for source, out in ((gated_in, gated_ref), (top_in, far_top), (low_in, far_low)):
            out[...] = source[...]


def end_part(begun, decay, start):
    mix, query, far, _, gated, top, low = begun
    return pl.pallas_call(
        end_kernel,
        out_shape=(short(*gated.shape), short(*top.shape), short(*low.shape)),
        in_specs=[VMEM] * 8,
        out_specs=(VMEM,) * 3,
        scratch_shapes=[pltpu.VMEM(mix.shape, jnp.float32)],
        compiler_params=params(),
        cost_estimate=cost(2**29, 2**20),
    )(mix, query, far, gated, top, low, decay, start)


def cut_rows(length, width):
    cut = length * CUT // 16
    return (cut, width), (length - cut, width)


def project(gated_ref, columns_ref, *outs):
    row = 0
    for out in outs:
        rows = slice(row, row + out.shape[0])
        out[...] = jnp.dot(
            gated_ref[rows, :], columns_ref[...], preferred_element_type=jnp.float32
        ).astype(out.dtype)
        row += out.shape[0]


def next_part(gated, columns):
    top, low = cut_rows(gated.shape[0], columns.shape[1])
    return pl.pallas_call(
        project,
        out_shape=(wide(*top), short(*low)),
        in_specs=[VMEM, VMEM],
        out_specs=(VMEM, VMEM),
        compiler_params=params(),
        cost_estimate=cost(2**29, 2**20),
    )(gated, columns)


def fetch_and_project(turn, gated_ref, weight_hbm, _, top_ref, low_ref, columns_ref, sems):
    wait_all(fetch_columns(weight_hbm, turn, columns_ref, sems))
    project(gated_ref, columns_ref, top_ref, low_ref)


def fetched_part(turn, out_shape, gated, weight, behind, ring):
    return pl.pallas_call(
        functools.partial(fetch_and_project, turn),
        out_shape=out_shape,
        in_specs=[VMEM, HBM, VMEM],
        out_specs=(VMEM, VMEM),
        scratch_shapes=[pltpu.VMEM((gated.shape[1], weight.shape[1] // ring), jnp.bfloat16), DMA((CHUNKS,))],
        compiler_params=params(),
        cost_estimate=cost(2**29, 2**21),
    )(gated, in_hbm(weight), behind)


def last_part(gated, weight, behind, ring):
    top, low = cut_rows(gated.shape[0], weight.shape[1] // ring)
    return fetched_part(LAST, (short(*top), wide(*low)), gated, weight, behind, ring)


def own_part(gated, weight, behind, ring):
    top, low = cut_rows(gated.shape[0], weight.shape[1] // ring)
    return fetched_part(MINE, (wide(*top), wide(*low)), gated, weight, behind, ring)


def finish_kernel(mine_top, near_top, both_top, mine_low, near_low, both_low, out_hbm, out_buf, sems):
    row = 0
    copies = []
    for mine, near, both in ((mine_top, near_top, both_top), (mine_low, near_low, both_low)):
        length = mine.shape[0]
        middle = length // (2 * ROWS) * ROWS
        for part in (slice(0, middle), slice(middle, length)):
            rows = pl.ds(row, part.stop - part.start)
            out_buf[rows, :] = (
                mine[part, :] + near[part, :].astype(jnp.float32) + both[part, :].astype(jnp.float32)
            ).astype(jnp.bfloat16)
            copies.append(
                pltpu.make_async_copy(out_buf.at[rows, :], out_hbm.at[rows, :], sems.at[len(copies)])
            )
            copies[-1].start()
            row += part.stop - part.start
    wait_all(copies)


def finish(*parts):
    length, width = parts[0].shape[0] + parts[3].shape[0], parts[0].shape[1]
    return pl.pallas_call(
        finish_kernel,
        out_shape=short(length, width),
        in_specs=[VMEM] * 6,
        out_specs=HBM,
        scratch_shapes=[pltpu.VMEM((length, width), jnp.bfloat16), DMA((4,))],
        compiler_params=params(),
        cost_estimate=cost(2**19, 2**21),
    )(*parts)


def scan_over_ctx(state, decay, length, index, work, load):
    devices = lax.axis_size("ctx")

    def power(blocks):
        blocks = jnp.asarray(blocks)
        reach = (length * jnp.maximum(blocks, 0)).astype(jnp.float32)
        return jnp.where(blocks >= 0, jnp.exp(-decay * reach), 0.0)

    total, before = state, jnp.zeros_like(state)
    span = 1
    for stage, (members, moves, forward) in enumerate(STAGES):
        mine, inside = index // span % members, index % span
        sent = total.astype(jnp.bfloat16)
        own = work(sent, members, span) if stage in WORK else power((members - 1 - mine) * span)
        if stage == len(STAGES) - 1:
            load(sent, before)
            before = jnp.zeros_like(state)
        got = []
        for k, flip in moves:
            pairs = [(i, i ^ flip) for i in range(devices)]
            if forward:
                pairs = [(i, j) for i, j in pairs if i < j]
            got.append((k, lax.ppermute(sent, "ctx", pairs).astype(jnp.float32)))
        total = total * own
        for k, theirs in got:
            other = mine ^ k
            before = before + theirs * power(
                jnp.where(other < mine, (mine - 1 - other) * span + inside, -1)
            )
            total = total + theirs * power((members - 1 - other) * span)
        span *= members
    return before


def on_device(gate_query, gate_key, value_in, residues, decay_rate, skip_gain, out_weight):
    index = lax.axis_index("ctx")
    length, chans = gate_key.shape
    groups = chans // LANES
    ring = lax.axis_size("tp")
    forth = [(i, (i + NEXT) % ring) for i in range(ring)]
    back = [(i, (i + LAST) % ring) for i in range(ring)]

    state, keyed, decay, residue, skip = block_state(
        gate_key, value_in, decay_rate.T, residues.T, skip_gain.reshape(groups, LANES)
    )
    scale = residue * jnp.sqrt(-jnp.expm1(-2.0 * decay))
    local, held = [], state

    def work(sent, members, apart):
        nonlocal held
        part, ahead, *left = local_part(len(local), members, apart, keyed, decay, scale, held, sent, skip)
        local.append(part)
        held = left[0] if left else held
        return ahead

    entry = scale * jnp.exp(-decay)

    def load(sent, before):
        nonlocal begun
        begun = begin_part(local, decay, entry * before, sent, gate_query, out_weight, ring)

    begun = None
    carry = scan_over_ctx(state, decay, length, index, work, load)
    gated, far_top, far_low = end_part(begun, decay, entry * carry)
    far_a = lax.ppermute(far_top, "tp", forth)
    far_b = lax.ppermute(far_low, "tp", back)
    next_top, next_low = next_part(gated, begun[3])
    near_b = lax.ppermute(next_low, "tp", forth)
    last_top, last_low = last_part(gated, out_weight, next_low, ring)
    near_a = lax.ppermute(last_top, "tp", back)
    mine_top, mine_low = own_part(gated, out_weight, last_top, ring)
    both_a = lax.ppermute((next_top + far_a.astype(jnp.float32)).astype(jnp.bfloat16), "tp", forth)
    both_b = lax.ppermute((last_low + far_b.astype(jnp.float32)).astype(jnp.bfloat16), "tp", back)
    return finish(mine_top, near_a, both_a, mine_low, near_b, both_b)


def solution(mesh):
    in_specs = (
        P("ctx", "tp"),
        P("ctx", "tp"),
        P("ctx", "tp"),
        P("tp", None),
        P("tp", None),
        P("tp"),
        P("tp", None),
    )
    return jax.shard_map(
        on_device, mesh=mesh, in_specs=in_specs, out_specs=P("ctx", "tp"), check_vma=False
    )
```
